256 devices in a mesh: fx: 8 (over y, core), fy: 8 (over z), col: 4 (over x).
Axes of the slice: x: 4, y: 4, z: 8, core: 2. Of those that a mesh axis runs over, the one named last changes fastest.
Arguments:
- x_velocity: bfloat16 [512, 512, 1024], P('fx', 'fy', 'col'), may hold values from -6 to 6
- y_velocity: bfloat16 [512, 512, 1024], P('fx', 'fy', 'col'), may hold values from -6 to 6
- z_velocity: bfloat16 [512, 512, 1024], P('fx', 'fy', 'col'), may hold values from -6 to 6
- source: bfloat16 [512, 512, 1024], P('fx', 'fy', 'col'), may hold values from -6 to 6
- coarse_adjoint: float32 [65536, 512], P(('fx', 'fy'), 'col'), may hold values from -6 to 6
- send_slot: int32 [65536], P(('fx', 'fy')), may hold values from 0 to 2047, as said below
- recv_index: int32 [65536], P(('fx', 'fy')), may hold values from 0 to 2047, as said below
Outputs:
- indicator: float32 [4, 65536], P('col', ('fx', 'fy'))
The draws below stay inside these ranges and needn't reach their ends.
Inputs may be any that keep to these rules, and one draw needn't show every extreme that they name: `send_slot`: within each device's block of 1024 entries, each value d * 32 + s names a slot s to device d of the fx, fy plane; no slot twice; every device sends at most 32 columns to one device, and some device sends exactly 32 to some device. `recv_index`: within each device's block of 1024 entries, each value o * 32 + s names the column that device o stores with send slot (this device) * 32 + s; every device receives exactly 1024 columns, each once.
All inputs are finite; a program needn't handle non-finite values.
Results may differ from the reference program's by a relative error of at most 0.0003.
Values may be sent and summed in bfloat16 or wider, within the bound.
A program may use at most 64 MiB of HBM per device.

```python
import math
import jax
import jax.numpy as jnp
from jax import lax

FX = 64
FY = 64
FZ = 256
PZ = 128
PENCILS = 1024
CAP = 32
NX = 512
NY = 512
NZ = 1024
N_FX = 8
N_FY = 8
N_COL = 4


def shuffled(subkey):
    return jax.random.permutation(subkey, PENCILS).astype(jnp.int32)


def routing(key):
    owners = N_FX * N_FY
    average = PENCILS // owners
    subkeys = jax.random.split(key, 6)
    spread = jax.random.randint(subkeys[0], (owners // 2,), 0, average + 1).astype(jnp.int32)
    spread = spread.at[0].set(average)
    loads = jnp.stack([average + spread, average - spread], axis=1).reshape(owners)
    loads = loads[jax.random.permutation(subkeys[1], owners)]
    shift_recv = jax.random.permutation(subkeys[2], owners).astype(jnp.int32)
    shift_send = jax.random.permutation(subkeys[3], owners).astype(jnp.int32)
    counts = loads[(shift_recv[None, :] - shift_send[:, None]) % owners]
    cumulative = jnp.cumsum(counts, axis=0)
    queue = jnp.arange(PENCILS, dtype=jnp.int32)
    sender = jnp.sum((cumulative.T[:, None, :] <= queue[None, :, None]).astype(jnp.int32), axis=2)
    recv_starts = (cumulative - counts).T
    within = queue[None, :] - jnp.take_along_axis(recv_starts, sender, axis=1)
    placing = jax.vmap(shuffled)(jax.random.split(subkeys[4], owners))
    receiver = jnp.broadcast_to(jnp.arange(owners, dtype=jnp.int32)[:, None], (owners, PENCILS))
    recv_table = jnp.zeros((owners, PENCILS), jnp.int32).at[receiver, placing].set(sender * CAP + within)
    row_starts = (jnp.cumsum(counts, axis=1) - counts).T
    raw_row = jnp.take_along_axis(row_starts, sender, axis=1) + within
    row_shuffle = jax.vmap(shuffled)(jax.random.split(subkeys[5], owners))
    final_row = row_shuffle[sender, raw_row]
    send_table = jnp.zeros((owners, PENCILS), jnp.int32).at[sender, final_row].set(receiver * CAP + within)
    return (send_table.reshape(-1), recv_table.reshape(-1))


def draw_send_slot(key, part):
    tables = routing(key)
    return tables[0]


def draw_recv_index(key, part):
    tables = routing(key)
    return tables[1]


def shard_levels(stream_key, dims, cuts, low, largest):
    level, own = 1.0, jax.random.fold_in(stream_key, 6)
    for position, blocks in cuts:
        draws = jnp.exp(jax.random.uniform(jax.random.fold_in(own, position), (blocks,), jnp.float32, low / len(cuts), largest / len(cuts)))
        level = level * jnp.repeat(draws, dims[position] // blocks).reshape([-1 if axis == position else 1 for axis in range(len(dims))])
    return level


def normal_values(own_key, shape, deviation, limit, cuts=(), kind=jnp.bfloat16):
    drawn = jax.random.normal(own_key, shape, jnp.float32) * deviation
    if len(cuts) > 0:
        drawn = shard_levels(own_key, shape, cuts, -0.22, 0.18) * drawn
    return jnp.clip(drawn, min=-limit, max=limit).astype(kind)


def setup_inputs(seed: int = 0) -> dict:
    streams_of = jax.random.split(jax.random.key(seed), 8)
    return {
        "x_velocity": normal_values(streams_of[0], (NX, NY, NZ), 1.0, 6.0, ((0, 8), (1, 8), (2, 4))),
        "y_velocity": normal_values(streams_of[1], (NX, NY, NZ), 1.0, 6.0, ((0, 8), (1, 8), (2, 4))),
        "z_velocity": normal_values(streams_of[2], (NX, NY, NZ), 1.0, 6.0, ((0, 8), (1, 8), (2, 4))),
        "source": normal_values(streams_of[3], (NX, NY, NZ), 1.0, 6.0, ((0, 8), (1, 8), (2, 4))),
        "coarse_adjoint": normal_values(streams_of[4], (N_FX * N_FY * PENCILS, N_COL * PZ), 1.0, 6.0, ((0, 64), (1, 4)), jnp.float32),
        "send_slot": draw_send_slot(jax.random.fold_in(streams_of[7], 71), 0),
        "recv_index": draw_recv_index(jax.random.fold_in(streams_of[7], 71), 0),
    }


def prolong_matrix(coarse_len):
    coarse_rows = jnp.arange(coarse_len, dtype=jnp.int32)[:, None]
    fine_cols = jnp.arange(2 * coarse_len, dtype=jnp.int32)[None, :]
    centre = fine_cols // 2
    beside = jnp.clip(centre + jnp.where(fine_cols % 2 == 0, -1, 1), 0, coarse_len - 1)
    return 0.75 * (coarse_rows == centre).astype(jnp.float32) + 0.25 * (coarse_rows == beside).astype(jnp.float32)

def pair_sums(x_velocity, y_velocity, z_velocity, source):

    def one_block(block):
        start = (block * FX).astype(jnp.int32)
        first_flow = lax.dynamic_slice_in_dim(x_velocity, start, FX, 0).astype(jnp.float32)
        following = jnp.minimum(start + FX, NX - 1).astype(jnp.int32)
        first_rim = lax.dynamic_slice_in_dim(x_velocity, following, 1, 0).astype(jnp.float32)
        first_rim = jnp.where(block < N_FX - 1, first_rim, jnp.float32(0.0))
        first_upper = jnp.concatenate([first_flow[1:], first_rim], 0)
        second_flow = lax.dynamic_slice_in_dim(y_velocity, start, FX, 0).astype(jnp.float32)
        second_upper = jnp.concatenate([second_flow[:, 1:], jnp.zeros_like(second_flow[:, :1])], 1)
        third_flow = lax.dynamic_slice_in_dim(z_velocity, start, FX, 0).astype(jnp.float32)
        third_upper = jnp.concatenate([third_flow[:, :, 1:], jnp.zeros_like(third_flow[:, :, :1])], 2)
        source_rows = lax.dynamic_slice_in_dim(source, start, FX, 0).astype(jnp.float32)
        residual = first_upper - first_flow + (second_upper - second_flow) + (third_upper - third_flow) - source_rows
        return residual.reshape(FX // 2, 2, NY // 2, 2, NZ).sum(axis=(1, 3))
    blocks = lax.map(one_block, jnp.arange(N_FX, dtype=jnp.int32))
    return blocks.reshape(NX // 2, NY // 2, NZ)

def reference(x_velocity, y_velocity, z_velocity, source, coarse_adjoint, send_slot, recv_index):
    owners = N_FX * N_FY
    total = owners * PENCILS
    stored = jnp.arange(total, dtype=jnp.int32)
    inverse = jnp.zeros((owners * owners * CAP,), jnp.int32)
    inverse = inverse.at[stored // PENCILS * (owners * CAP) + send_slot].set(stored)
    receiver = stored // PENCILS
    home = inverse[recv_index // CAP * (owners * CAP) + receiver * CAP + recv_index % CAP]
    gathered = coarse_adjoint[home].reshape(total, N_COL, PZ)
    weights = jnp.einsum('nck,kf->ncf', gathered, prolong_matrix(PZ), precision=lax.Precision.HIGHEST)
    sums = pair_sums(x_velocity, y_velocity, z_velocity, source)
    sums = sums.reshape(N_FX, FX // 2, N_FY, FY // 2, N_COL, FZ).transpose(0, 2, 1, 3, 4, 5).reshape(total, N_COL, FZ)
    values = lax.optimization_barrier(jnp.sum(sums * weights, axis=-1)) * (1.0 / math.sqrt(4 * FZ))
    return jnp.zeros((N_COL, total), jnp.float32).at[:, home].set(values.T)
```

```python
import functools
import math

import jax
import jax.numpy as jnp
from jax import lax
from jax.experimental import pallas as pl
from jax.experimental.pallas import tpu as pltpu
from jax.sharding import PartitionSpec as P

MESH = pl.DeviceIdType.MESH
F32 = jnp.float32
BF16 = jnp.bfloat16
I32 = jnp.int32
LIMIT = 32766.0
STEPS = 64.0


def iota(shape, axis):
    return lax.broadcasted_iota(I32, shape, axis)


def restriction(fine_len, coarse_len, shift):
    fine = iota((fine_len, coarse_len), 0) - shift
    coarse = iota((fine_len, coarse_len), 1)
    centre = lax.shift_right_arithmetic(fine, 1)
    odd = fine & 1
    beside = jnp.clip(centre + 2 * odd - 1, 0, coarse_len - 1)
    weight = jnp.where(coarse == centre, 0.75, 0.0) + jnp.where(coarse == beside, 0.25, 0.0)
    return jnp.where(fine >= 0, weight, 0.0).astype(F32)


def split(value):
    high = value.astype(BF16)
    return high, (value - high.astype(F32)).astype(BF16)


def slots_of(index_ref, chunk, table):
    slot = chunk * 256 + iota((256, 128), 0)
    hot = [
        jnp.where(index_ref[a : a + 1, :] == slot, 1.0, 0.0).astype(BF16) for a in range(8)
    ]
    both = jnp.dot(jnp.concatenate(hot, axis=1), table[...], preferred_element_type=F32)
    return both[:, :128] + both[:, 128:]


def exchange(
    n_fx,
    n_fy,
    n_col,
    x_hbm,
    y_hbm,
    z_hbm,
    s_hbm,
    adj_hbm,
    recv_hbm,
    slot_hbm,
    dots_ref,
    xb,
    yb,
    zb,
    sb,
    adjb,
    recvb,
    slotb,
    xrim,
    yrim,
    zrim,
    ysend,
    zsend,
    zc,
    xm,
    bb,
    ry,
    table,
    table2,
    adjs,
    msg,
    got,
    in_sem,
    small_sem,
    rim_send,
    rim_recv,
    send_sem,
    recv_sem,
    row_sem,
):
    fx, fy, col = lax.axis_index("fx"), lax.axis_index("fy"), lax.axis_index("col")
    me = fx * n_fy + fy
    fx_before, fy_before = lax.rem(fx + n_fx - 1, n_fx), lax.rem(fy + n_fy - 1, n_fy)
    col_before, col_after = lax.rem(col + n_col - 1, n_col), lax.rem(col + 1, n_col)

    small = [
        pltpu.make_async_copy(recv_hbm, recvb, small_sem.at[0]),
        pltpu.make_async_copy(slot_hbm, slotb, small_sem.at[1]),
        pltpu.make_async_copy(adj_hbm, adjb, small_sem.at[2]),
    ]

    def inputs(g):
        return [
            pltpu.make_async_copy(y_hbm.at[g], yb.at[g], in_sem.at[0, g]),
            pltpu.make_async_copy(z_hbm.at[g], zb.at[g], in_sem.at[1, g]),
            pltpu.make_async_copy(x_hbm.at[g, :, 0], xb.at[g], in_sem.at[2, g]),
            pltpu.make_async_copy(s_hbm.at[g], sb.at[g], in_sem.at[3, g]),
        ]

    def start_yz(g, _):
        for copy in inputs(g)[:2]:
            copy.start()
        return 0

    def start_xs(g, _):
        for copy in inputs(g)[2:]:
            copy.start()
        return 0

    lax.fori_loop(0, 8, start_yz, 0)

    barrier = pltpu.get_barrier_semaphore()

    def announce(k, _):
        pl.semaphore_signal(barrier, inc=1, device_id=(lax.rem(fx + k, n_fx), fy, col), device_id_type=MESH)
        pl.semaphore_signal(barrier, inc=1, device_id=(fx, lax.rem(fy + k, n_fy), col), device_id_type=MESH)
        return 0

    lax.fori_loop(1, 8, announce, 0)
    pl.semaphore_signal(barrier, inc=1, device_id=(fx, fy, col_before), device_id_type=MESH)
    pl.semaphore_signal(barrier, inc=1, device_id=(fx, fy, col_after), device_id_type=MESH)

    lax.fori_loop(0, 8, start_xs, 0)
    for copy in small:
        copy.start()

    below = restriction(256, 128, 0)
    third = (restriction(256, 128, 1) - below).astype(BF16)
    below = below.astype(BF16)
    first_cell = jnp.where(iota((256, 128), 0) == 0, 1.0, 0.0).astype(BF16)
    third = jnp.concatenate([third, first_cell], axis=1)
    lane64 = iota((64, 128), 1)

    zc[...] = jnp.zeros_like(zc)

    def fine_yz(g, _):
        for copy in inputs(g)[:2]:
            copy.wait()
        yy = jnp.dot(yb[g, :, 0].reshape(256, 256), below, preferred_element_type=F32) + jnp.dot(
            yb[g, :, 1].reshape(256, 256), below, preferred_element_type=F32
        )
        zz = jnp.dot(zb[g, :, 0].reshape(256, 256), third, preferred_element_type=F32) + jnp.dot(
            zb[g, :, 1].reshape(256, 256), third, preferred_element_type=F32
        )
        bb[pl.ds(pl.multiple_of(g * 256, 256), 256), :] = zz[:, :128]
        edge = zc[...]
        for ii in range(4):
            i = g * 4 + ii
            block = yy[ii * 64 : ii * 64 + 64]
            ry[pl.ds(pl.multiple_of(i * 72, 8), 64), :] = block
            ysend[i] = block[0:1]
            edge = edge + jnp.where(lane64 == i, zz[ii * 64 : ii * 64 + 64, 128:], 0.0)
        zc[...] = edge
        return 0

    lax.fori_loop(0, 8, fine_yz, 0)
    zsend[...] = zc[pl.ds(0, 32, stride=2), :] + zc[pl.ds(1, 32, stride=2), :]

    pl.semaphore_wait(barrier, 2 * 7 + 2)

    def tell_column(k, _):
        pl.semaphore_signal(row_sem, inc=1, device_id=(fx, lax.rem(fy + k, n_fy), col), device_id_type=MESH)
        return 0

    lax.fori_loop(1, 8, tell_column, 0)
    rims = [
        pltpu.make_async_remote_copy(
            src_ref=x_hbm.at[0, 0, 0],
            dst_ref=xrim,
            send_sem=rim_send.at[0],
            recv_sem=rim_recv.at[0],
            device_id=(fx_before, fy, col),
            device_id_type=MESH,
        ),
        pltpu.make_async_remote_copy(
            src_ref=ysend,
            dst_ref=yrim,
            send_sem=rim_send.at[1],
            recv_sem=rim_recv.at[1],
            device_id=(fx, fy_before, col),
            device_id_type=MESH,
        ),
        pltpu.make_async_remote_copy(
            src_ref=zsend,
            dst_ref=zrim,
            send_sem=rim_send.at[2],
            recv_sem=rim_recv.at[2],
            device_id=(fx, fy, col_before),
            device_id_type=MESH,
        ),
    ]
    for copy in rims:
        copy.start()

    def fine_xs(g, _):
        for copy in inputs(g)[2:]:
            copy.wait()
        xx = jnp.dot(xb[g].reshape(256, 256), below, preferred_element_type=F32)
        ss = jnp.dot(sb[g, :, 0].reshape(256, 256), below, preferred_element_type=F32) + jnp.dot(
            sb[g, :, 1].reshape(256, 256), below, preferred_element_type=F32
        )
        rows = pl.ds(pl.multiple_of(g * 256, 256), 256)
        xm[rows, :] = xx
        bb[rows, :] = bb[rows, :] - xx - ss
        return 0

    lax.fori_loop(0, 8, fine_xs, 0)
    for copy in small:
        copy.wait()
    for copy in rims:
        copy.wait()
    inner_x = jnp.where(fx < n_fx - 1, 1.0, 0.0)
    inner_y = jnp.where(fy < n_fy - 1, 1.0, 0.0)
    inner_z = jnp.where(col < n_col - 1, 1.0, 0.0)
    xm[2048:2112, :] = inner_x * jnp.dot(xrim[...], below, preferred_element_type=F32)
    for i in range(32):
        ry[i * 72 + 64 : i * 72 + 65, :] = inner_y * yrim[i]
    last = iota((32, 128), 1) == 127
    zlast = inner_z * zrim[...]

    def finish(g, _):
        base = pl.multiple_of(g * 256, 256)
        total = (
            bb[pl.ds(base, 128, stride=2), :]
            + bb[pl.ds(base + 1, 128, stride=2), :]
            + xm[pl.ds(base + 64, 128, stride=2), :]
            + xm[pl.ds(base + 65, 128, stride=2), :]
        )
        parts = []
        for ii in range(4):
            i = g * 4 + ii
            row = pl.multiple_of(i * 72, 8)
            part = ry[pl.ds(row + 2, 32, stride=2), :] - ry[pl.ds(row, 32, stride=2), :]
            parts.append(part + jnp.where(last, pltpu.roll(zlast, 127 - i, 1), 0.0))
        total = total + jnp.concatenate(parts, axis=0)
        high, mid = split(total)
        rows = pl.ds(pl.multiple_of(g * 128, 128), 128)
        table[rows, 0:128] = high
        table[rows, 128:256] = mid
        return 0

    lax.fori_loop(0, 8, finish, 0)
    pl.semaphore_wait(row_sem, 7)

    place = iota((8, 32, 128), 2) == iota((8, 32, 128), 1) + 32 * lax.rem(fy, 4)

    def pack(t, first):
        c = lax.rem(fx + 1 + t, n_fx)
        value = slots_of(recvb, c, table)
        largest = jnp.max(jnp.abs(value), axis=1, keepdims=True)
        level = jnp.ceil(jnp.log2(jnp.maximum(largest, 1e-33)) * STEPS) + 1.0
        code = jnp.floor(value * (jnp.exp2(level * (-1.0 / STEPS)) * LIMIT) + 0.5).astype(I32)
        code = code.reshape(8, 32, 128)
        word = lax.shift_left(code[:, 0:16], 16) | (code[:, 16:32] & 0xFFFF)
        msg[pl.ds(c * 8, 8), 0:16, :] = word
        level = jnp.where(place, level.reshape(8, 32, 1), 0.0)
        msg[pl.ds(c * 8, 8), 16:17, :] = jnp.sum(level, axis=1, keepdims=True).astype(I32)

        def send(k, _):
            to = lax.rem(fy + k, n_fy)
            pltpu.make_async_remote_copy(
                src_ref=msg.at[c * 8 + to],
                dst_ref=got.at[me],
                send_sem=send_sem,
                recv_sem=recv_sem.at[me],
                device_id=(c, to, col),
                device_id_type=MESH,
            ).start()
            return 0

        lax.fori_loop(first, 8, send, 0)

    def pack_step(t, _):
        pack(t, 0)
        return 0

    lax.fori_loop(0, 7, pack_step, 0)
    pack(7, 1)
    got[me] = msg[me]

    high, mid = split(adjb[...])
    table2[:, 0:128] = high
    table2[:, 128:256] = mid

    def place_adjoint(c, _):
        adjs[pl.ds(c * 8, 8)] = slots_of(slotb, c, table2).reshape(8, 32, 128)
        return 0

    lax.fori_loop(0, 8, place_adjoint, 0)

    diagonal = iota((2, 128, 128), 1) == iota((2, 128, 128), 2)

    def take(t, skip):
        c = lax.rem(fx + 2 * n_fx - 1 - t, n_fx)

        def arrived(k, _):
            o = c * 8 + lax.rem(fy + n_fy - k, n_fy)
            pltpu.make_async_copy(got.at[o], got.at[o], recv_sem.at[o]).wait()
            return 0

        lax.fori_loop(skip, 8, arrived, 0)
        word = got[pl.ds(c * 8, 8), 0:16, :]
        upper = lax.shift_right_arithmetic(word, 16).astype(F32)
        lower = lax.shift_right_arithmetic(lax.shift_left(word, 16), 16).astype(F32)
        columns = adjs[pl.ds(c * 8, 8)]
        product = jnp.concatenate([upper, lower], axis=1) * columns
        dot = jnp.sum(product, axis=2, keepdims=True).reshape(2, 128, 1)
        dot = jnp.sum(jnp.where(diagonal, dot, 0.0), axis=1)
        level = got[pl.ds(c * 8, 8), 16:17, :].astype(F32).reshape(2, 4, 128)
        level = jnp.sum(level, axis=1)
        dots_ref[c] = dot * (jnp.exp2(level * (1.0 / STEPS)) * (1.0 / (LIMIT * math.sqrt(4 * 256))))

    def take_step(t, _):
        take(t, 0)
        return 0

    lax.fori_loop(0, 7, take_step, 0)
    take(7, 1)
    sent = msg.at[pl.ds(0, 63)]
    pltpu.make_async_copy(sent, sent, send_sem).wait()


def pick(dots_ref, slot_ref, out_ref):
    slot = slot_ref[...]
    lane = slot & 127
    row = lax.shift_right_logical(slot, 7)
    out = jnp.zeros((8, 128), F32)
    for r in range(16):
        source = jnp.broadcast_to(dots_ref[r // 2, r % 2 : r % 2 + 1, :], (8, 128))
        out = jnp.where(row == r, jnp.take_along_axis(source, lane, axis=1), out)
    out_ref[...] = out


def per_device(x_velocity, y_velocity, z_velocity, source, coarse_adjoint, send_slot, recv_index):
    n_fx, n_fy, n_col = lax.axis_size("fx"), lax.axis_size("fy"), lax.axis_size("col")
    any_spec = pl.BlockSpec(memory_space=pl.ANY)
    vmem = pl.BlockSpec(memory_space=pltpu.VMEM)
    shape5 = (8, 4, 2, 64, 256)
    dma = pltpu.SemaphoreType.DMA
    dots = pl.pallas_call(
        functools.partial(exchange, n_fx, n_fy, n_col),
        out_shape=jax.ShapeDtypeStruct((8, 2, 128), F32),
        in_specs=[any_spec] * 7,
        out_specs=vmem,
        scratch_shapes=[
            pltpu.VMEM((8, 4, 64, 256), BF16),
            pltpu.VMEM(shape5, BF16),
            pltpu.VMEM(shape5, BF16),
            pltpu.VMEM(shape5, BF16),
            pltpu.VMEM((1024, 128), F32),
            pltpu.VMEM((8, 128), I32),
            pltpu.VMEM((8, 128), I32),
            pltpu.VMEM((64, 256), BF16),
            pltpu.VMEM((32, 1, 128), F32),
            pltpu.VMEM((32, 128), F32),
            pltpu.VMEM((32, 1, 128), F32),
            pltpu.VMEM((32, 128), F32),
            pltpu.VMEM((64, 128), F32),
            pltpu.VMEM((2112, 128), F32),
            pltpu.VMEM((2048, 128), F32),
            pltpu.VMEM((32 * 72, 128), F32),
            pltpu.VMEM((1024, 256), BF16),
            pltpu.VMEM((1024, 256), BF16),
            pltpu.VMEM((64, 32, 128), F32),
            pltpu.VMEM((64, 17, 128), I32),
            pltpu.VMEM((64, 17, 128), I32),
            dma((4, 8)),
            dma((3,)),
            dma((3,)),
            dma((3,)),
            dma,
            dma((64,)),
            pltpu.SemaphoreType.REGULAR,
        ],
        compiler_params=pltpu.CompilerParams(
            collective_id=0, has_side_effects=True, vmem_limit_bytes=56 * 1024 * 1024
        ),
    )(
        x_velocity.reshape(shape5),
        y_velocity.reshape(shape5),
        z_velocity.reshape(shape5),
        source.reshape(shape5),
        coarse_adjoint,
        recv_index.reshape(8, 128),
        send_slot.reshape(8, 128),
    )
    out = pl.pallas_call(
        pick,
        out_shape=jax.ShapeDtypeStruct((8, 128), F32),
        in_specs=[vmem, vmem],
        out_specs=vmem,
    )(dots, send_slot.reshape(8, 128))
    return out.reshape(1, 1024)


def solution(mesh):
    return jax.shard_map(
        per_device,
        mesh=mesh,
        in_specs=(
            P("fx", "fy", "col"),
            P("fx", "fy", "col"),
            P("fx", "fy", "col"),
            P("fx", "fy", "col"),
            P(("fx", "fy"), "col"),
            P(("fx", "fy")),
            P(("fx", "fy")),
        ),
        out_specs=P("col", ("fx", "fy")),
        check_vma=False,
    )
```

```python
import functools
import math

import jax
import jax.numpy as jnp
from jax import lax
from jax.experimental import pallas as pl
from jax.experimental.pallas import tpu as pltpu
from jax.sharding import PartitionSpec as P

MESH = pl.DeviceIdType.MESH
F32 = jnp.float32
BF16 = jnp.bfloat16
I32 = jnp.int32
LIMIT = 32766.0
STEPS = 64.0


def iota(shape, axis):
    return lax.broadcasted_iota(I32, shape, axis)


def restriction(fine_len, coarse_len):
    fine = iota((fine_len, coarse_len), 0)
    coarse = iota((fine_len, coarse_len), 1)
    centre = lax.shift_right_logical(fine, 1)
    beside = jnp.clip(centre + 2 * (fine & 1) - 1, 0, coarse_len - 1)
    return jnp.where(coarse == centre, 0.75, 0.0) + jnp.where(coarse == beside, 0.25, 0.0)


def split(value):
    high = value.astype(BF16)
    return high, (value - high.astype(F32)).astype(BF16)


def slots_of(index_ref, first, second, table):
    row = iota((512, 128), 0)
    fx = jnp.where(row < 256, first, second)
    slot = fx * 256 + (row & 255)
    hot = [
        jnp.where(index_ref[a : a + 1, :] == slot, 1.0, 0.0).astype(BF16) for a in range(8)
    ]
    both = jnp.dot(jnp.concatenate(hot, axis=1), table[...], preferred_element_type=F32)
    return both[:, :128] + both[:, 128:]


def exchange(
    n_fx,
    n_fy,
    n_col,
    x_hbm,
    y_hbm,
    z_hbm,
    s_hbm,
    adj_hbm,
    recv_hbm,
    slot_hbm,
    dots_ref,
    xb,
    yb,
    zb,
    sb,
    adjb,
    recvb,
    slotb,
    yrim,
    zrim,
    yfirst,
    ysend,
    zsend,
    ye,
    ze,
    xs,
    zlow,
    sums,
    restricted,
    edge_rows,
    table,
    table2,
    adjs,
    msg,
    got,
    edge_sem,
    in_sem,
    small_sem,
    rim_send,
    rim_recv,
    send_sem,
    recv_sem,
    row_sem,
):
    fx, fy, col = lax.axis_index("fx"), lax.axis_index("fy"), lax.axis_index("col")
    here = fx * n_fy + fy
    fx_before, fy_before = ((fx + n_fx - 1) & 7), ((fy + n_fy - 1) & 7)
    col_before, col_after = ((col + n_col - 1) & 3), ((col + 1) & 3)

    def remote(src, dst, send, recv, to_fx, to_fy, to_col=col):
        return pltpu.make_async_remote_copy(
            src_ref=src, dst_ref=dst, send_sem=send, recv_sem=recv, device_id=(to_fx, to_fy, to_col), device_id_type=MESH
        )

    small = [
        pltpu.make_async_copy(recv_hbm, recvb, small_sem.at[0]),
        pltpu.make_async_copy(slot_hbm, slotb, small_sem.at[1]),
        pltpu.make_async_copy(adj_hbm, adjb, small_sem.at[2]),
    ]

    edge_y = pltpu.make_async_copy(y_hbm.at[:, :, :, 0:16], yb.at[:, :, :, 0:16], edge_sem.at[0])
    edge_z = pltpu.make_async_copy(z_hbm.at[:, :, :, :, 0:128], zb.at[0], edge_sem.at[1])

    def input_x(g):
        return pltpu.make_async_copy(x_hbm.at[g, :, 0], xb.at[pl.ds(8 * g, 8)], in_sem.at[2, g])

    def inputs(g):
        return [
            pltpu.make_async_copy(y_hbm.at[g, :, :, 16:64], yb.at[g, :, :, 16:64], in_sem.at[0, g]),
            pltpu.make_async_copy(z_hbm.at[g, :, :, :, 128:256], zb.at[1, g], in_sem.at[1, g]),
            pltpu.make_async_copy(s_hbm.at[g], sb.at[g], in_sem.at[3, g]),
        ]


    barrier = pltpu.get_barrier_semaphore()

    def announce(k, _):
        pl.semaphore_signal(barrier, inc=1, device_id=(fx, ((fy + k) & 7), col), device_id_type=MESH)
        pl.semaphore_signal(barrier, inc=1, device_id=(((fx + k) & 7), fy, col), device_id_type=MESH)
        return 0

    for k in range(1, 8):
        announce(k, 0)
    pl.semaphore_signal(barrier, inc=1, device_id=(fx, fy, col_before), device_id_type=MESH)
    pl.semaphore_signal(barrier, inc=1, device_id=(fx, fy, col_after), device_id_type=MESH)

    edge_y.start()
    edge_z.start()
    input_x(0).start()
    for g in range(4):
        if g < 3:
            input_x(g + 1).start()
        for copy in inputs(g):
            copy.start()
    for copy in small:
        copy.start()

    def tell_column(k, _):
        pl.semaphore_signal(row_sem, inc=1, device_id=(fx, ((fy + k) & 7), col), device_id_type=MESH)
        return 0

    rim_x = remote(x_hbm.at[0, 0, 0], xb.at[32], rim_send.at[0], rim_recv.at[0], fx_before, fy)
    rim_y = remote(ysend, yrim, rim_send.at[1], rim_recv.at[1], fx, fy_before)
    rim_z = remote(zsend, zrim, rim_send.at[2], rim_recv.at[2], fx, fy, col_before)

    def pair(t):
        return ((fx + 1 + 2 * t) & 7), ((fx + 2 + 2 * t) & 7)

    place = iota((8, 32, 128), 2) == iota((8, 32, 128), 1) + 32 * (fy & 3)

    def encode(value, first, second):
        largest = jnp.max(jnp.abs(value), axis=1, keepdims=True)
        level = jnp.ceil(jnp.log2(jnp.maximum(largest, 1e-33)) * STEPS) + 1.0
        code = jnp.floor(value * (jnp.exp2(level * (-1.0 / STEPS)) * LIMIT) + 0.5).astype(I32)
        code = code.reshape(16, 32, 128)
        word = lax.shift_left(code[:, 0:16], 16) | (code[:, 16:32] & 0xFFFF)
        level = level.reshape(16, 32, 1)
        for u, f in enumerate((first, second)):
            msg[pl.ds(f * 8, 8), 0:16, :] = word[u * 8 : u * 8 + 8]
            row = jnp.sum(jnp.where(place, level[u * 8 : u * 8 + 8], 0.0), axis=1, keepdims=True)
            msg[pl.ds(f * 8, 8), 16:17, :] = row.astype(I32)

    def send_rows(t, first, second):
        def one(f, k):
            to = (fy + k) & 7
            remote(msg.at[f * 8 + to], got.at[here], send_sem, recv_sem.at[here], f, to).start()

        for k in range(8):
            one(first, k)
        pl.when(t < 3)(lambda: one(second, 0))
        for k in range(1, 8):
            one(second, k)

    def wait_rows(f, own):
        def one(k):
            o = f * 8 + ((fy + k) & 7)
            pltpu.make_async_copy(got.at[o], got.at[o], recv_sem.at[o]).wait()

        if own is None:
            one(0)
        else:
            pl.when(jnp.logical_not(own))(lambda: one(0))
        for k in range(1, 8):
            one(k)

    def dots_of(f, columns):
        word = got[pl.ds(f * 8, 8), 0:16, :]
        upper = lax.shift_right_arithmetic(word, 16).astype(F32)
        lower = lax.shift_right_arithmetic(lax.shift_left(word, 16), 16).astype(F32)
        product = jnp.concatenate([upper, lower], axis=1) * columns
        return jnp.sum(product, axis=2, keepdims=True), got[pl.ds(f * 8, 8), 16:17, :].astype(F32)

    pl.semaphore_wait(barrier, 2 * 7 + 2)
    for k in range(1, 8):
        tell_column(k, 0)
    rim_x.start()

    below = restriction(256, 128).astype(BF16)
    below2 = jnp.concatenate([below, below], axis=0)

    lane = iota((32, 128), 1)
    halves = [slice(0, 128), slice(128, 256)]
    ye[...] = jnp.zeros_like(ye)
    edge_y.wait()
    for i in range(32):
        rows = yb[i // 8, i % 8, :, 0:16, :].astype(F32)
        yfirst[i : i + 1, :] = rows[0, 0:1] + rows[1, 0:1]
    high, mid = split(yfirst[...])
    ysend[...] = jnp.dot(jnp.concatenate([high, mid], axis=1), below2, preferred_element_type=F32)
    rim_y.start()
    edge_z.wait()
    zsend[...] = jnp.zeros_like(zsend)

    def fine_z(g, _):
        for ii in range(8):
            ze[ii, 0] = zb[0, g, ii, 0].astype(F32) + zb[0, g, ii, 1].astype(F32)
        edge = zsend[...]
        for ii in range(8):
            z = ze[ii, 0, pl.ds(0, 32, stride=2), :] + ze[ii, 0, pl.ds(1, 32, stride=2), :]
            edge = jnp.where(lane == g * 8 + ii, z[:, 0:1], edge)
            zlow[g * 8 + ii] = z
        zsend[...] = edge
        return 0

    for g in range(4):
        fine_z(g, 0)
    rim_z.start()


    def fine(g, _):
        if g == 0:
            input_x(0).wait()
        if g < 3:
            input_x(g + 1).wait()
        for copy in inputs(g):
            copy.wait()
        if g == 3:
            rim_x.wait()
            xb[32] = jnp.where(fx < n_fx - 1, xb[32], jnp.zeros_like(xb[32]))

        for ii in range(8):
            i = g * 8 + ii
            for h in range(2):
                ye[ii, h, 0:64] = yb[g, ii, 0, :, halves[h]].astype(F32) + yb[g, ii, 1, :, halves[h]].astype(F32)
                lower = xb[i, :, halves[h]].astype(F32) + sb[g, ii, 0, :, halves[h]].astype(F32)
                upper = xb[i + 1, :, halves[h]].astype(F32) - sb[g, ii, 1, :, halves[h]].astype(F32)
                xs[ii, h] = upper - lower
            ze[ii, 1] = zb[1, g, ii, 0].astype(F32) + zb[1, g, ii, 1].astype(F32)
        for ii in range(8):
            i = g * 8 + ii
            z0 = zlow[i]
            z1 = ze[ii, 1, pl.ds(0, 32, stride=2), :] + ze[ii, 1, pl.ds(1, 32, stride=2), :]
            next0, next1 = pltpu.roll(z0, 127, 1), pltpu.roll(z1, 127, 1)
            next0 = jnp.where(lane == 127, next1, next0)
            next1 = jnp.where(lane == 127, 0.0, next1)
            rows = pl.ds(g * 256 + ii * 32, 32)
            for h, change in enumerate((next0 - z0, next1 - z1)):
                rise = ye[ii, h, pl.ds(2, 32, stride=2), :] - ye[ii, h, pl.ds(0, 32, stride=2), :]
                rest = xs[ii, h, pl.ds(0, 32, stride=2), :] + xs[ii, h, pl.ds(1, 32, stride=2), :]
                high, mid = split(change + rise + rest)
                sums[rows, h * 128 : h * 128 + 128] = high
                sums[rows, 256 + h * 128 : 256 + h * 128 + 128] = mid
        rows = pl.ds(g * 256, 256)
        restricted[rows, :] = jnp.dot(sums[rows, :], below2, preferred_element_type=F32)
        return 0

    for g in range(4):
        fine(g, 0)
    small[0].wait()
    rim_y.wait()
    rim_z.wait()
    inner_y = jnp.where(fy < n_fy - 1, 1.0, 0.0)
    inner_z = jnp.where(col < n_col - 1, 1.0, 0.0)
    edge_rows[...] = inner_y * yrim[...]
    zlast = inner_z * zrim[...]
    bottom = iota((8, 128), 0) == 7

    def finish(g, _):
        for ii in range(8):
            i = g * 8 + ii
            rows = pl.ds(g * 256 + ii * 32, 32)
            total = restricted[rows, :] + jnp.where(lane == 127, pltpu.roll(zlast, 127 - i, 1), 0.0)
            row = jnp.where(bottom, edge_rows[pl.ds(i, 1), :], 0.0)
            total = jnp.concatenate([total[:24], total[24:] + row], axis=0)
            high, mid = split(total)
            table[rows, 0:128] = high
            table[rows, 128:256] = mid
        return 0

    for g in range(4):
        finish(g, 0)

    def send_residuals(t, _):
        first, second = pair(t)
        encode(slots_of(recvb, first, second, table), first, second)

        @pl.when(t == 0)
        def _():
            pl.semaphore_wait(row_sem, 7)

        send_rows(t, first, second)
        return 0

    lax.fori_loop(0, 4, send_residuals, 0)
    got[here] = msg[here]

    small[1].wait()
    small[2].wait()
    high, mid = split(adjb[...])
    table2[:, 0:128] = high
    table2[:, 128:256] = mid
    def place_columns(t, _):
        first, second = ((fx + 15 - 2 * t) & 7), ((fx + 14 - 2 * t) & 7)
        adjs[t] = slots_of(slotb, first, second, table2).reshape(2, 8, 32, 128)
        return 0

    lax.fori_loop(0, 4, place_columns, 0)
    diagonal = iota((2, 128, 128), 1) == iota((2, 128, 128), 2)
    norm = 1.0 / (LIMIT * math.sqrt(4 * 256))

    def take_rows(t, _):
        for u, f in enumerate((((fx + 15 - 2 * t) & 7), ((fx + 14 - 2 * t) & 7))):
            wait_rows(f, t == 3 if u == 1 else None)
            dot, level = dots_of(f, adjs[t, u])
            dot = jnp.sum(jnp.where(diagonal, dot.reshape(2, 128, 1), 0.0), axis=1)
            level = jnp.sum(level.reshape(2, 4, 128), axis=1)
            dots_ref[f] = dot * (jnp.exp2(level * (1.0 / STEPS)) * norm)
        return 0

    lax.fori_loop(0, 4, take_rows, 0)

    sent = msg.at[pl.ds(0, 63)]
    pltpu.make_async_copy(sent, sent, send_sem).wait()


def pick(dots_ref, slot_ref, out_ref):
    slot = slot_ref[...]
    lane = slot & 127
    row = lax.shift_right_logical(slot, 7)
    out = jnp.zeros((8, 128), F32)
    for r in range(16):
        source = jnp.broadcast_to(dots_ref[r // 2, r % 2 : r % 2 + 1, :], (8, 128))
        out = jnp.where(row == r, jnp.take_along_axis(source, lane, axis=1), out)
    out_ref[...] = out


def per_device(x_velocity, y_velocity, z_velocity, source, coarse_adjoint, send_slot, recv_index):
    n_fx, n_fy, n_col = lax.axis_size("fx"), lax.axis_size("fy"), lax.axis_size("col")
    any_spec = pl.BlockSpec(memory_space=pl.ANY)
    vmem = pl.BlockSpec(memory_space=pltpu.VMEM)
    shape5 = (4, 8, 2, 64, 256)
    dma = pltpu.SemaphoreType.DMA
    dots = pl.pallas_call(
        functools.partial(exchange, n_fx, n_fy, n_col),
        out_shape=jax.ShapeDtypeStruct((8, 2, 128), F32),
        in_specs=[any_spec] * 7,
        out_specs=vmem,
        scratch_shapes=[
            pltpu.VMEM((33, 64, 256), BF16),
            pltpu.VMEM(shape5, BF16),
            pltpu.VMEM((2, 4, 8, 2, 64, 128), BF16),
            pltpu.VMEM(shape5, BF16),
            pltpu.VMEM((1024, 128), F32),
            pltpu.VMEM((8, 128), I32),
            pltpu.VMEM((8, 128), I32),
            pltpu.VMEM((32, 128), F32),
            pltpu.VMEM((32, 128), F32),
            pltpu.VMEM((32, 256), F32),
            pltpu.VMEM((32, 128), F32),
            pltpu.VMEM((32, 128), F32),
            pltpu.VMEM((8, 2, 72, 128), F32),
            pltpu.VMEM((8, 2, 64, 128), F32),
            pltpu.VMEM((8, 2, 64, 128), F32),
            pltpu.VMEM((32, 32, 128), F32),
            pltpu.VMEM((1024, 512), BF16),
            pltpu.VMEM((1024, 128), F32),
            pltpu.VMEM((32, 128), F32),
            pltpu.VMEM((1024, 256), BF16),
            pltpu.VMEM((1024, 256), BF16),
            pltpu.VMEM((4, 2, 8, 32, 128), F32),
            pltpu.VMEM((64, 17, 128), I32),
            pltpu.VMEM((64, 17, 128), I32),
            dma((2,)),
            dma((4, 4)),
            dma((3,)),
            dma((3,)),
            dma((3,)),
            dma,
            dma((64,)),
            pltpu.SemaphoreType.REGULAR,
        ],
        compiler_params=pltpu.CompilerParams(
            collective_id=0, has_side_effects=True, vmem_limit_bytes=56 * 1024 * 1024
        ),
    )(
        x_velocity.reshape(shape5),
        y_velocity.reshape(shape5),
        z_velocity.reshape(shape5),
        source.reshape(shape5),
        coarse_adjoint,
        recv_index.reshape(8, 128),
        send_slot.reshape(8, 128),
    )
    out = pl.pallas_call(
        pick,
        out_shape=jax.ShapeDtypeStruct((8, 128), F32),
        in_specs=[vmem, vmem],
        out_specs=vmem,
    )(dots, send_slot.reshape(8, 128))
    return out.reshape(1, 1024)


def solution(mesh):
    return jax.shard_map(
        per_device,
        mesh=mesh,
        in_specs=(
            P("fx", "fy", "col"),
            P("fx", "fy", "col"),
            P("fx", "fy", "col"),
            P("fx", "fy", "col"),
            P(("fx", "fy"), "col"),
            P(("fx", "fy")),
            P(("fx", "fy")),
        ),
        out_specs=P("col", ("fx", "fy")),
        check_vma=False,
    )
```

```python
import functools
import math

import jax
import jax.numpy as jnp
from jax import lax
from jax.experimental import pallas as pl
from jax.experimental.pallas import tpu as pltpu
from jax.sharding import PartitionSpec as P

MESH = pl.DeviceIdType.MESH
F32 = jnp.float32
BF16 = jnp.bfloat16
I32 = jnp.int32
LIMIT = 32766.0
STEPS = 64.0


def iota(shape, axis):
    return lax.broadcasted_iota(I32, shape, axis)


def restriction(fine_len, coarse_len):
    fine = iota((fine_len, coarse_len), 0)
    coarse = iota((fine_len, coarse_len), 1)
    centre = lax.shift_right_logical(fine, 1)
    beside = jnp.clip(centre + 2 * (fine & 1) - 1, 0, coarse_len - 1)
    return jnp.where(coarse == centre, 0.75, 0.0) + jnp.where(coarse == beside, 0.25, 0.0)


def split(value):
    high = value.astype(BF16)
    return high, (value - high.astype(F32)).astype(BF16)


def slots_of(index_ref, first, second, table):
    row = iota((512, 128), 0)
    fx = jnp.where(row < 256, first, second)
    slot = fx * 256 + (row & 255)
    hot = [
        jnp.where(index_ref[a : a + 1, :] == slot, 1.0, 0.0).astype(BF16) for a in range(8)
    ]
    both = jnp.dot(jnp.concatenate(hot, axis=1), table[...], preferred_element_type=F32)
    return both[:, :128] + both[:, 128:]


def exchange(
    n_fx,
    n_fy,
    n_col,
    x_hbm,
    y_hbm,
    z_hbm,
    s_hbm,
    adj_hbm,
    recv_hbm,
    slot_hbm,
    dots_ref,
    xb,
    yb,
    zb,
    sb,
    adjb,
    recvb,
    slotb,
    yrim,
    zrim,
    yfirst,
    ysend,
    zsend,
    ye,
    ze,
    xs,
    zlow,
    sums,
    restricted,
    edge_rows,
    table,
    table2,
    adjs,
    msg,
    got,
    edge_sem,
    in_sem,
    small_sem,
    rim_send,
    rim_recv,
    send_sem,
    recv_sem,
    row_sem,
):
    fx, fy, col = lax.axis_index("fx"), lax.axis_index("fy"), lax.axis_index("col")
    here = fx * n_fy + fy
    fx_before, fy_before = ((fx + n_fx - 1) & 7), ((fy + n_fy - 1) & 7)
    col_before, col_after = ((col + n_col - 1) & 3), ((col + 1) & 3)

    def remote(src, dst, send, recv, to_fx, to_fy, to_col=col):
        return pltpu.make_async_remote_copy(
            src_ref=src, dst_ref=dst, send_sem=send, recv_sem=recv, device_id=(to_fx, to_fy, to_col), device_id_type=MESH
        )

    small = [
        pltpu.make_async_copy(recv_hbm, recvb, small_sem.at[0]),
        pltpu.make_async_copy(slot_hbm, slotb, small_sem.at[1]),
        pltpu.make_async_copy(adj_hbm, adjb, small_sem.at[2]),
    ]

    edge_y = pltpu.make_async_copy(y_hbm.at[:, :, :, 0:16], yb.at[:, :, :, 0:16], edge_sem.at[0])
    edge_z = pltpu.make_async_copy(z_hbm.at[:, :, :, :, 0:128], zb.at[0], edge_sem.at[1])

    def input_x(g):
        return pltpu.make_async_copy(x_hbm.at[g, :, 0], xb.at[pl.ds(8 * g, 8)], in_sem.at[2, g])

    def inputs(g):
        return [
            pltpu.make_async_copy(y_hbm.at[g, :, :, 16:64], yb.at[g, :, :, 16:64], in_sem.at[0, g]),
            pltpu.make_async_copy(z_hbm.at[g, :, :, :, 128:256], zb.at[1, g], in_sem.at[1, g]),
            pltpu.make_async_copy(s_hbm.at[g], sb.at[g], in_sem.at[3, g]),
        ]


    barrier = pltpu.get_barrier_semaphore()

    def announce(k, _):
        pl.semaphore_signal(barrier, inc=1, device_id=(fx, ((fy + k) & 7), col), device_id_type=MESH)
        pl.semaphore_signal(barrier, inc=1, device_id=(((fx + k) & 7), fy, col), device_id_type=MESH)
        return 0

    for k in range(1, 8):
        announce(k, 0)
    pl.semaphore_signal(barrier, inc=1, device_id=(fx, fy, col_before), device_id_type=MESH)
    pl.semaphore_signal(barrier, inc=1, device_id=(fx, fy, col_after), device_id_type=MESH)

    edge_y.start()
    edge_z.start()
    input_x(0).start()
    for g in range(4):
        if g < 3:
            input_x(g + 1).start()
        for copy in inputs(g):
            copy.start()
    for copy in small:
        copy.start()

    def tell_column(k, _):
        pl.semaphore_signal(row_sem, inc=1, device_id=(fx, ((fy + k) & 7), col), device_id_type=MESH)
        return 0

    rim_x = remote(x_hbm.at[0, 0, 0], xb.at[32], rim_send.at[0], rim_recv.at[0], fx_before, fy)
    rim_y = remote(ysend, yrim, rim_send.at[1], rim_recv.at[1], fx, fy_before)
    rim_z = remote(zsend, zrim, rim_send.at[2], rim_recv.at[2], fx, fy, col_before)

    def pair(t):
        return ((fx + 1 + 2 * t) & 7), ((fx + 2 + 2 * t) & 7)

    place = iota((8, 32, 128), 2) == iota((8, 32, 128), 1) + 32 * (fy & 3)

    def encode(value, first, second):
        largest = jnp.max(jnp.abs(value), axis=1, keepdims=True)
        level = jnp.ceil(jnp.log2(jnp.maximum(largest, 1e-33)) * STEPS) + 1.0
        code = jnp.floor(value * (jnp.exp2(level * (-1.0 / STEPS)) * LIMIT) + 0.5).astype(I32)
        code = code.reshape(16, 32, 128)
        word = lax.shift_left(code[:, 0:16], 16) | (code[:, 16:32] & 0xFFFF)
        level = level.reshape(16, 32, 1)
        for u, f in enumerate((first, second)):
            msg[pl.ds(f * 8, 8), 0:16, :] = word[u * 8 : u * 8 + 8]
            row = jnp.sum(jnp.where(place, level[u * 8 : u * 8 + 8], 0.0), axis=1, keepdims=True)
            msg[pl.ds(f * 8, 8), 16:17, :] = row.astype(I32)

    def send_rows(t, first, second):
        def one(f, k):
            to = (fy + k) & 7
            remote(msg.at[f * 8 + to], got.at[here], send_sem, recv_sem.at[here], f, to).start()

        for k in range(8):
            one(first, k)
        pl.when(t < 3)(lambda: one(second, 0))
        for k in range(1, 8):
            one(second, k)

    def wait_rows(f, own):
        def one(k):
            o = f * 8 + ((fy + k) & 7)
            pltpu.make_async_copy(got.at[o], got.at[o], recv_sem.at[o]).wait()

        if own is None:
            one(0)
        else:
            pl.when(jnp.logical_not(own))(lambda: one(0))
        for k in range(1, 8):
            one(k)

    def dots_of(f, columns):
        word = got[pl.ds(f * 8, 8), 0:16, :]
        upper = lax.shift_right_arithmetic(word, 16).astype(F32)
        lower = lax.shift_right_arithmetic(lax.shift_left(word, 16), 16).astype(F32)
        product = jnp.concatenate([upper, lower], axis=1) * columns
        return jnp.sum(product, axis=2, keepdims=True), got[pl.ds(f * 8, 8), 16:17, :].astype(F32)

    pl.semaphore_wait(barrier, 2 * 7 + 2)
    for k in range(1, 8):
        tell_column(k, 0)
    rim_x.start()

    below = restriction(256, 128).astype(BF16)
    below2 = jnp.concatenate([below, below], axis=0)

    lane = iota((32, 128), 1)
    halves = [slice(0, 128), slice(128, 256)]
    ye[...] = jnp.zeros_like(ye)
    edge_y.wait()
    for i in range(32):
        rows = yb[i // 8, i % 8, :, 0:16, :].astype(F32)
        yfirst[i : i + 1, :] = rows[0, 0:1] + rows[1, 0:1]
    high, mid = split(yfirst[...])
    ysend[...] = jnp.dot(jnp.concatenate([high, mid], axis=1), below2, preferred_element_type=F32)
    rim_y.start()
    edge_z.wait()
    zsend[...] = jnp.zeros_like(zsend)

    def fine_z(g, _):
        for ii in range(8):
            ze[ii, 0] = zb[0, g, ii, 0].astype(F32) + zb[0, g, ii, 1].astype(F32)
        edge = zsend[...]
        for ii in range(8):
            z = ze[ii, 0, pl.ds(0, 32, stride=2), :] + ze[ii, 0, pl.ds(1, 32, stride=2), :]
            edge = jnp.where(lane == g * 8 + ii, z[:, 0:1], edge)
            zlow[g * 8 + ii] = z
        zsend[...] = edge
        return 0

    for g in range(4):
        fine_z(g, 0)
    rim_z.start()


    def fine(g, _):
        if g == 0:
            input_x(0).wait()
        if g < 3:
            input_x(g + 1).wait()
        for copy in inputs(g):
            copy.wait()
        if g == 3:
            rim_x.wait()
            xb[32] = jnp.where(fx < n_fx - 1, xb[32], jnp.zeros_like(xb[32]))

        for ii in range(8):
            i = g * 8 + ii
            for h in range(2):
                ye[ii, h, 0:64] = yb[g, ii, 0, :, halves[h]].astype(F32) + yb[g, ii, 1, :, halves[h]].astype(F32)
                lower = xb[i, :, halves[h]].astype(F32) + sb[g, ii, 0, :, halves[h]].astype(F32)
                upper = xb[i + 1, :, halves[h]].astype(F32) - sb[g, ii, 1, :, halves[h]].astype(F32)
                xs[ii, h] = upper - lower
            ze[ii, 1] = zb[1, g, ii, 0].astype(F32) + zb[1, g, ii, 1].astype(F32)
        for ii in range(8):
            i = g * 8 + ii
            z0 = zlow[i]
            z1 = ze[ii, 1, pl.ds(0, 32, stride=2), :] + ze[ii, 1, pl.ds(1, 32, stride=2), :]
            next0, next1 = pltpu.roll(z0, 127, 1), pltpu.roll(z1, 127, 1)
            next0 = jnp.where(lane == 127, next1, next0)
            next1 = jnp.where(lane == 127, 0.0, next1)
            rows = pl.ds(g * 256 + ii * 32, 32)
            for h, change in enumerate((next0 - z0, next1 - z1)):
                rise = ye[ii, h, pl.ds(2, 32, stride=2), :] - ye[ii, h, pl.ds(0, 32, stride=2), :]
                rest = xs[ii, h, pl.ds(0, 32, stride=2), :] + xs[ii, h, pl.ds(1, 32, stride=2), :]
                high, mid = split(change + rise + rest)
                sums[rows, h * 128 : h * 128 + 128] = high
                sums[rows, 256 + h * 128 : 256 + h * 128 + 128] = mid
        rows = pl.ds(g * 256, 256)
        restricted[rows, :] = jnp.dot(sums[rows, :], below2, preferred_element_type=F32)
        return 0

    for g in range(4):
        fine(g, 0)
    small[0].wait()
    rim_y.wait()
    rim_z.wait()
    inner_y = jnp.where(fy < n_fy - 1, 1.0, 0.0)
    inner_z = jnp.where(col < n_col - 1, 1.0, 0.0)
    edge_rows[...] = inner_y * yrim[...]
    zlast = inner_z * zrim[...]
    bottom = iota((8, 128), 0) == 7

    def finish(g, _):
        for ii in range(8):
            i = g * 8 + ii
            rows = pl.ds(g * 256 + ii * 32, 32)
            total = restricted[rows, :] + jnp.where(lane == 127, pltpu.roll(zlast, 127 - i, 1), 0.0)
            row = jnp.where(bottom, edge_rows[pl.ds(i, 1), :], 0.0)
            total = jnp.concatenate([total[:24], total[24:] + row], axis=0)
            high, mid = split(total)
            table[rows, 0:128] = high
            table[rows, 128:256] = mid
        return 0

    for g in range(4):
        finish(g, 0)

    def send_residuals(t, _):
        first, second = pair(t)
        encode(slots_of(recvb, first, second, table), first, second)

        @pl.when(t == 0)
        def _():
            pl.semaphore_wait(row_sem, 7)

        send_rows(t, first, second)
        return 0

    lax.fori_loop(0, 4, send_residuals, 0)
    got[here] = msg[here]

    small[1].wait()
    small[2].wait()
    high, mid = split(adjb[...])
    table2[:, 0:128] = high
    table2[:, 128:256] = mid
    def place_columns(t, _):
        first, second = ((fx + 15 - 2 * t) & 7), ((fx + 14 - 2 * t) & 7)
        adjs[t] = slots_of(slotb, first, second, table2).reshape(2, 8, 32, 128)
        return 0

    lax.fori_loop(0, 4, place_columns, 0)
    diagonal = iota((2, 128, 128), 1) == iota((2, 128, 128), 2)
    norm = 1.0 / (LIMIT * math.sqrt(4 * 256))

    def take_rows(t, _):
        for u, f in enumerate((((fx + 15 - 2 * t) & 7), ((fx + 14 - 2 * t) & 7))):
            wait_rows(f, t == 3 if u == 1 else None)
            dot, level = dots_of(f, adjs[t, u])
            dot = jnp.sum(jnp.where(diagonal, dot.reshape(2, 128, 1), 0.0), axis=1)
            level = jnp.sum(level.reshape(2, 4, 128), axis=1)
            dots_ref[f] = dot * (jnp.exp2(level * (1.0 / STEPS)) * norm)
        return 0

    lax.fori_loop(0, 4, take_rows, 0)

    sent = msg.at[pl.ds(0, 63)]
    pltpu.make_async_copy(sent, sent, send_sem).wait()


def pick(dots_ref, slot_ref, out_ref):
    slot = slot_ref[...]
    lane = slot & 127
    row = lax.shift_right_logical(slot, 7)
    out = jnp.zeros((8, 128), F32)
    for r in range(16):
        source = jnp.broadcast_to(dots_ref[r // 2, r % 2 : r % 2 + 1, :], (8, 128))
        out = jnp.where(row == r, jnp.take_along_axis(source, lane, axis=1), out)
    out_ref[...] = out


def per_device(x_velocity, y_velocity, z_velocity, source, coarse_adjoint, send_slot, recv_index):
    n_fx, n_fy, n_col = lax.axis_size("fx"), lax.axis_size("fy"), lax.axis_size("col")
    any_spec = pl.BlockSpec(memory_space=pl.ANY)
    vmem = pl.BlockSpec(memory_space=pltpu.VMEM)
    shape5 = (4, 8, 2, 64, 256)
    dma = pltpu.SemaphoreType.DMA
    dots = pl.pallas_call(
        functools.partial(exchange, n_fx, n_fy, n_col),
        out_shape=pltpu.VMEM((8, 2, 128), F32),
        in_specs=[any_spec] * 7,
        out_specs=vmem,
        scratch_shapes=[
            pltpu.VMEM((33, 64, 256), BF16),
            pltpu.VMEM(shape5, BF16),
            pltpu.VMEM((2, 4, 8, 2, 64, 128), BF16),
            pltpu.VMEM(shape5, BF16),
            pltpu.VMEM((1024, 128), F32),
            pltpu.VMEM((8, 128), I32),
            pltpu.VMEM((8, 128), I32),
            pltpu.VMEM((32, 128), F32),
            pltpu.VMEM((32, 128), F32),
            pltpu.VMEM((32, 256), F32),
            pltpu.VMEM((32, 128), F32),
            pltpu.VMEM((32, 128), F32),
            pltpu.VMEM((8, 2, 72, 128), F32),
            pltpu.VMEM((8, 2, 64, 128), F32),
            pltpu.VMEM((8, 2, 64, 128), F32),
            pltpu.VMEM((32, 32, 128), F32),
            pltpu.VMEM((1024, 512), BF16),
            pltpu.VMEM((1024, 128), F32),
            pltpu.VMEM((32, 128), F32),
            pltpu.VMEM((1024, 256), BF16),
            pltpu.VMEM((1024, 256), BF16),
            pltpu.VMEM((4, 2, 8, 32, 128), F32),
            pltpu.VMEM((64, 17, 128), I32),
            pltpu.VMEM((64, 17, 128), I32),
            dma((2,)),
            dma((4, 4)),
            dma((3,)),
            dma((3,)),
            dma((3,)),
            dma,
            dma((64,)),
            pltpu.SemaphoreType.REGULAR,
        ],
        compiler_params=pltpu.CompilerParams(
            collective_id=0, has_side_effects=True, vmem_limit_bytes=58720256
        ),
    )(
        x_velocity.reshape(shape5),
        y_velocity.reshape(shape5),
        z_velocity.reshape(shape5),
        source.reshape(shape5),
        coarse_adjoint,
        recv_index.reshape(8, 128),
        send_slot.reshape(8, 128),
    )
    out = pl.pallas_call(
        pick,
        out_shape=jax.ShapeDtypeStruct((8, 128), F32),
        in_specs=[vmem, vmem],
        out_specs=vmem,
        compiler_params=pltpu.CompilerParams(vmem_limit_bytes=1024 * 1024),
    )(dots, send_slot.reshape(8, 128))
    return out.reshape(1, 1024)


def solution(mesh):
    return jax.shard_map(
        per_device,
        mesh=mesh,
        in_specs=(
            P("fx", "fy", "col"),
            P("fx", "fy", "col"),
            P("fx", "fy", "col"),
            P("fx", "fy", "col"),
            P(("fx", "fy"), "col"),
            P(("fx", "fy")),
            P(("fx", "fy")),
        ),
        out_specs=P("col", ("fx", "fy")),
        check_vma=False,
    )
```

```python
import functools
import math

import jax
import jax.numpy as jnp
from jax import lax
from jax.experimental import pallas as pl
from jax.experimental.pallas import tpu as pltpu
from jax.sharding import PartitionSpec as P

MESH = pl.DeviceIdType.MESH
F32 = jnp.float32
BF16 = jnp.bfloat16
I32 = jnp.int32
LIMIT = 32766.0
STEPS = 64.0


def iota(shape, axis):
    return lax.broadcasted_iota(I32, shape, axis)


def restriction(fine_len, coarse_len):
    fine = iota((fine_len, coarse_len), 0)
    coarse = iota((fine_len, coarse_len), 1)
    centre = lax.shift_right_logical(fine, 1)
    beside = jnp.clip(centre + 2 * (fine & 1) - 1, 0, coarse_len - 1)
    return jnp.where(coarse == centre, 0.75, 0.0) + jnp.where(coarse == beside, 0.25, 0.0)


def split(value):
    high = value.astype(BF16)
    return high, (value - high.astype(F32)).astype(BF16)


def slots_of(index_ref, first, second, table):
    row = iota((256 if second is None else 512, 128), 0)
    fx = first if second is None else jnp.where(row < 256, first, second)
    slot = fx * 256 + (row & 255)
    hot = [
        jnp.where(index_ref[a : a + 1, :] == slot, 1.0, 0.0).astype(BF16) for a in range(8)
    ]
    both = jnp.dot(jnp.concatenate(hot, axis=1), table[...], preferred_element_type=F32)
    return both[:, :128] + both[:, 128:]


def exchange(
    n_fx,
    n_fy,
    n_col,
    x_hbm,
    y_hbm,
    z_hbm,
    s_hbm,
    adj_hbm,
    recv_hbm,
    slot_hbm,
    dots_ref,
    xb,
    yb,
    zb,
    sb,
    adjb,
    recvb,
    slotb,
    yrim,
    zrim,
    yfirst,
    ysend,
    zsend,
    ye,
    ze,
    xs,
    zlow,
    sums,
    restricted,
    edge_rows,
    table,
    table2,
    adjs,
    msg,
    got,
    edge_sem,
    in_sem,
    small_sem,
    rim_send,
    rim_recv,
    send_sem,
    recv_sem,
    row_sem,
):
    fx, fy, col = lax.axis_index("fx"), lax.axis_index("fy"), lax.axis_index("col")
    here = fx * n_fy + fy
    fx_before, fy_before = ((fx + n_fx - 1) & 7), ((fy + n_fy - 1) & 7)
    col_before, col_after = ((col + n_col - 1) & 3), ((col + 1) & 3)

    def remote(src, dst, send, recv, to_fx, to_fy, to_col=col):
        return pltpu.make_async_remote_copy(
            src_ref=src, dst_ref=dst, send_sem=send, recv_sem=recv, device_id=(to_fx, to_fy, to_col), device_id_type=MESH
        )

    small = [
        pltpu.make_async_copy(recv_hbm, recvb, small_sem.at[0]),
        pltpu.make_async_copy(slot_hbm, slotb, small_sem.at[1]),
        pltpu.make_async_copy(adj_hbm, adjb, small_sem.at[2]),
    ]

    edge_y = pltpu.make_async_copy(y_hbm.at[:, :, :, 0:16], yb.at[:, :, :, 0:16], edge_sem.at[0])
    edge_z = pltpu.make_async_copy(z_hbm.at[:, :, :, :, 0:128], zb.at[0], edge_sem.at[1])

    def input_x(g):
        return pltpu.make_async_copy(x_hbm.at[g, :, 0], xb.at[pl.ds(8 * g, 8)], in_sem.at[2, g])

    def inputs(g):
        return [
            pltpu.make_async_copy(y_hbm.at[g, :, :, 16:64], yb.at[g, :, :, 16:64], in_sem.at[0, g]),
            pltpu.make_async_copy(z_hbm.at[g, :, :, :, 128:256], zb.at[1, g], in_sem.at[1, g]),
            pltpu.make_async_copy(s_hbm.at[g], sb.at[g], in_sem.at[3, g]),
        ]


    barrier = pltpu.get_barrier_semaphore()

    def announce(k, _):
        pl.semaphore_signal(barrier, inc=1, device_id=(fx, ((fy + k) & 7), col), device_id_type=MESH)
        pl.semaphore_signal(barrier, inc=1, device_id=(((fx + k) & 7), fy, col), device_id_type=MESH)
        return 0

    for k in range(1, 8):
        announce(k, 0)
    pl.semaphore_signal(barrier, inc=1, device_id=(fx, fy, col_before), device_id_type=MESH)
    pl.semaphore_signal(barrier, inc=1, device_id=(fx, fy, col_after), device_id_type=MESH)

    edge_y.start()
    edge_z.start()
    input_x(0).start()
    for g in range(4):
        if g < 3:
            input_x(g + 1).start()
        for copy in inputs(g):
            copy.start()
    for copy in small:
        copy.start()

    def tell_column(k, _):
        pl.semaphore_signal(row_sem, inc=1, device_id=(fx, ((fy + k) & 7), col), device_id_type=MESH)
        return 0

    rim_x = remote(x_hbm.at[0, 0, 0], xb.at[32], rim_send.at[0], rim_recv.at[0], fx_before, fy)
    rim_y = remote(ysend, yrim, rim_send.at[1], rim_recv.at[1], fx, fy_before)
    rim_z = remote(zsend, zrim, rim_send.at[2], rim_recv.at[2], fx, fy, col_before)

    def pair(t):
        return ((fx + 1 + 2 * t) & 7), ((fx + 2 + 2 * t) & 7)

    place = iota((8, 32, 128), 2) == iota((8, 32, 128), 1) + 32 * (fy & 3)

    def encode(value, first, second):
        largest = jnp.max(jnp.abs(value), axis=1, keepdims=True)
        level = jnp.ceil(jnp.log2(jnp.maximum(largest, 1e-33)) * STEPS) + 1.0
        code = jnp.floor(value * (jnp.exp2(level * (-1.0 / STEPS)) * LIMIT) + 0.5).astype(I32)
        code = code.reshape(-1, 32, 128)
        word = lax.shift_left(code[:, 0:16], 16) | (code[:, 16:32] & 0xFFFF)
        level = level.reshape(-1, 32, 1)
        for u, f in enumerate((first,) if second is None else (first, second)):
            msg[pl.ds(f * 8, 8), 0:16, :] = word[u * 8 : u * 8 + 8]
            row = jnp.sum(jnp.where(place, level[u * 8 : u * 8 + 8], 0.0), axis=1, keepdims=True)
            msg[pl.ds(f * 8, 8), 16:17, :] = row.astype(I32)

    def send_row(f, k):
        to = (fy + k) & 7
        remote(msg.at[f * 8 + to], got.at[here], send_sem, recv_sem.at[here], f, to).start()

    def send_rows(t, first, second):
        for k in range(8):
            send_row(first, k)
        pl.when(t < 3)(lambda: send_row(second, 0))
        for k in range(1, 8):
            send_row(second, k)

    def wait_rows(f, own):
        def one(k):
            o = f * 8 + ((fy + k) & 7)
            pltpu.make_async_copy(got.at[o], got.at[o], recv_sem.at[o]).wait()

        if own is None:
            one(0)
        else:
            pl.when(jnp.logical_not(own))(lambda: one(0))
        for k in range(1, 8):
            one(k)

    def dots_of(f, columns):
        word = got[pl.ds(f * 8, 8), 0:16, :]
        upper = lax.shift_right_arithmetic(word, 16).astype(F32)
        lower = lax.shift_right_arithmetic(lax.shift_left(word, 16), 16).astype(F32)
        product = jnp.concatenate([upper, lower], axis=1) * columns
        return jnp.sum(product, axis=2, keepdims=True), got[pl.ds(f * 8, 8), 16:17, :].astype(F32)

    pl.semaphore_wait(barrier, 2 * 7 + 2)
    for k in range(1, 8):
        tell_column(k, 0)
    rim_x.start()

    below = restriction(256, 128).astype(BF16)
    below2 = jnp.concatenate([below, below], axis=0)

    lane = iota((32, 128), 1)
    halves = [slice(0, 128), slice(128, 256)]
    ye[...] = jnp.zeros_like(ye)
    edge_y.wait()
    for i in range(32):
        rows = yb[i // 8, i % 8, :, 0:16, :].astype(F32)
        yfirst[i : i + 1, :] = rows[0, 0:1] + rows[1, 0:1]
    high, mid = split(yfirst[...])
    ysend[...] = jnp.dot(jnp.concatenate([high, mid], axis=1), below2, preferred_element_type=F32)
    rim_y.start()
    edge_z.wait()
    zsend[...] = jnp.zeros_like(zsend)

    def fine_z(g, _):
        for ii in range(8):
            ze[ii, 0] = zb[0, g, ii, 0].astype(F32) + zb[0, g, ii, 1].astype(F32)
        edge = zsend[...]
        for ii in range(8):
            z = ze[ii, 0, pl.ds(0, 32, stride=2), :] + ze[ii, 0, pl.ds(1, 32, stride=2), :]
            edge = jnp.where(lane == g * 8 + ii, z[:, 0:1], edge)
            zlow[g * 8 + ii] = z
        zsend[...] = edge
        return 0

    for g in range(4):
        fine_z(g, 0)
    rim_z.start()


    def fine(g, _):
        if g == 0:
            input_x(0).wait()
        if g < 3:
            input_x(g + 1).wait()
        for copy in inputs(g):
            copy.wait()
        if g == 3:
            rim_x.wait()
            xb[32] = jnp.where(fx < n_fx - 1, xb[32], jnp.zeros_like(xb[32]))

        for ii in range(8):
            i = g * 8 + ii
            for h in range(2):
                ye[ii, h, 0:64] = yb[g, ii, 0, :, halves[h]].astype(F32) + yb[g, ii, 1, :, halves[h]].astype(F32)
                lower = xb[i, :, halves[h]].astype(F32) + sb[g, ii, 0, :, halves[h]].astype(F32)
                upper = xb[i + 1, :, halves[h]].astype(F32) - sb[g, ii, 1, :, halves[h]].astype(F32)
                xs[ii, h] = upper - lower
            ze[ii, 1] = zb[1, g, ii, 0].astype(F32) + zb[1, g, ii, 1].astype(F32)
        for ii in range(8):
            i = g * 8 + ii
            z0 = zlow[i]
            z1 = ze[ii, 1, pl.ds(0, 32, stride=2), :] + ze[ii, 1, pl.ds(1, 32, stride=2), :]
            next0, next1 = pltpu.roll(z0, 127, 1), pltpu.roll(z1, 127, 1)
            next0 = jnp.where(lane == 127, next1, next0)
            next1 = jnp.where(lane == 127, 0.0, next1)
            rows = pl.ds(g * 256 + ii * 32, 32)
            for h, change in enumerate((next0 - z0, next1 - z1)):
                rise = ye[ii, h, pl.ds(2, 32, stride=2), :] - ye[ii, h, pl.ds(0, 32, stride=2), :]
                rest = xs[ii, h, pl.ds(0, 32, stride=2), :] + xs[ii, h, pl.ds(1, 32, stride=2), :]
                high, mid = split(change + rise + rest)
                sums[rows, h * 128 : h * 128 + 128] = high
                sums[rows, 256 + h * 128 : 256 + h * 128 + 128] = mid
        rows = pl.ds(g * 256, 256)
        restricted[rows, :] = jnp.dot(sums[rows, :], below2, preferred_element_type=F32)
        return 0

    for g in range(4):
        fine(g, 0)
    small[0].wait()
    rim_y.wait()
    rim_z.wait()
    inner_y = jnp.where(fy < n_fy - 1, 1.0, 0.0)
    inner_z = jnp.where(col < n_col - 1, 1.0, 0.0)
    edge_rows[...] = inner_y * yrim[...]
    zlast = inner_z * zrim[...]
    bottom = iota((8, 128), 0) == 7

    def finish(g, _):
        for ii in range(8):
            i = g * 8 + ii
            rows = pl.ds(g * 256 + ii * 32, 32)
            total = restricted[rows, :] + jnp.where(lane == 127, pltpu.roll(zlast, 127 - i, 1), 0.0)
            row = jnp.where(bottom, edge_rows[pl.ds(i, 1), :], 0.0)
            total = jnp.concatenate([total[:24], total[24:] + row], axis=0)
            high, mid = split(total)
            table[rows, 0:128] = high
            table[rows, 128:256] = mid
        return 0

    for g in range(4):
        finish(g, 0)

    def send_residuals(t, _):
        first, second = pair(t)
        encode(slots_of(recvb, first, second, table), first, second)
        send_rows(t, first, second)
        return 0

    for u, f in enumerate(pair(0)):
        encode(slots_of(recvb, f, None, table), f, None)
        if u == 0:
            pl.semaphore_wait(row_sem, 7)
        for k in range(8):
            send_row(f, k)
    lax.fori_loop(1, 4, send_residuals, 0)
    got[here] = msg[here]

    small[1].wait()
    small[2].wait()
    high, mid = split(adjb[...])
    table2[:, 0:128] = high
    table2[:, 128:256] = mid
    def place_columns(t, _):
        first, second = ((fx + 15 - 2 * t) & 7), ((fx + 14 - 2 * t) & 7)
        adjs[t] = slots_of(slotb, first, second, table2).reshape(2, 8, 32, 128)
        return 0

    lax.fori_loop(0, 4, place_columns, 0)
    diagonal = iota((2, 128, 128), 1) == iota((2, 128, 128), 2)
    norm = 1.0 / (LIMIT * math.sqrt(4 * 256))

    def take_rows(t, _):
        for u, f in enumerate((((fx + 15 - 2 * t) & 7), ((fx + 14 - 2 * t) & 7))):
            wait_rows(f, t == 3 if u == 1 else None)
            dot, level = dots_of(f, adjs[t, u])
            dot = jnp.sum(jnp.where(diagonal, dot.reshape(2, 128, 1), 0.0), axis=1)
            level = jnp.sum(level.reshape(2, 4, 128), axis=1)
            dots_ref[f] = dot * (jnp.exp2(level * (1.0 / STEPS)) * norm)
        return 0

    lax.fori_loop(0, 4, take_rows, 0)

    sent = msg.at[pl.ds(0, 63)]
    pltpu.make_async_copy(sent, sent, send_sem).wait()


def pick(dots_ref, slot_ref, out_ref):
    slot = slot_ref[...]
    lane = slot & 127
    row = lax.shift_right_logical(slot, 7)
    out = jnp.zeros((8, 128), F32)
    for r in range(16):
        source = jnp.broadcast_to(dots_ref[r // 2, r % 2 : r % 2 + 1, :], (8, 128))
        out = jnp.where(row == r, jnp.take_along_axis(source, lane, axis=1), out)
    out_ref[...] = out


def per_device(x_velocity, y_velocity, z_velocity, source, coarse_adjoint, send_slot, recv_index):
    n_fx, n_fy, n_col = lax.axis_size("fx"), lax.axis_size("fy"), lax.axis_size("col")
    any_spec = pl.BlockSpec(memory_space=pl.ANY)
    vmem = pl.BlockSpec(memory_space=pltpu.VMEM)
    shape5 = (4, 8, 2, 64, 256)
    dma = pltpu.SemaphoreType.DMA
    dots = pl.pallas_call(
        functools.partial(exchange, n_fx, n_fy, n_col),
        out_shape=pltpu.VMEM((8, 2, 128), F32),
        in_specs=[any_spec] * 7,
        out_specs=vmem,
        scratch_shapes=[
            pltpu.VMEM((33, 64, 256), BF16),
            pltpu.VMEM(shape5, BF16),
            pltpu.VMEM((2, 4, 8, 2, 64, 128), BF16),
            pltpu.VMEM(shape5, BF16),
            pltpu.VMEM((1024, 128), F32),
            pltpu.VMEM((8, 128), I32),
            pltpu.VMEM((8, 128), I32),
            pltpu.VMEM((32, 128), F32),
            pltpu.VMEM((32, 128), F32),
            pltpu.VMEM((32, 256), F32),
            pltpu.VMEM((32, 128), F32),
            pltpu.VMEM((32, 128), F32),
            pltpu.VMEM((8, 2, 72, 128), F32),
            pltpu.VMEM((8, 2, 64, 128), F32),
            pltpu.VMEM((8, 2, 64, 128), F32),
            pltpu.VMEM((32, 32, 128), F32),
            pltpu.VMEM((1024, 512), BF16),
            pltpu.VMEM((1024, 128), F32),
            pltpu.VMEM((32, 128), F32),
            pltpu.VMEM((1024, 256), BF16),
            pltpu.VMEM((1024, 256), BF16),
            pltpu.VMEM((4, 2, 8, 32, 128), F32),
            pltpu.VMEM((64, 17, 128), I32),
            pltpu.VMEM((64, 17, 128), I32),
            dma((2,)),
            dma((4, 4)),
            dma((3,)),
            dma((3,)),
            dma((3,)),
            dma,
            dma((64,)),
            pltpu.SemaphoreType.REGULAR,
        ],
        compiler_params=pltpu.CompilerParams(
            collective_id=0, has_side_effects=True, vmem_limit_bytes=58720256
        ),
    )(
        x_velocity.reshape(shape5),
        y_velocity.reshape(shape5),
        z_velocity.reshape(shape5),
        source.reshape(shape5),
        coarse_adjoint,
        recv_index.reshape(8, 128),
        send_slot.reshape(8, 128),
    )
    out = pl.pallas_call(
        pick,
        out_shape=jax.ShapeDtypeStruct((8, 128), F32),
        in_specs=[vmem, vmem],
        out_specs=vmem,
        compiler_params=pltpu.CompilerParams(vmem_limit_bytes=1024 * 1024),
    )(dots, send_slot.reshape(8, 128))
    return out.reshape(1, 1024)


def solution(mesh):
    return jax.shard_map(
        per_device,
        mesh=mesh,
        in_specs=(
            P("fx", "fy", "col"),
            P("fx", "fy", "col"),
            P("fx", "fy", "col"),
            P("fx", "fy", "col"),
            P(("fx", "fy"), "col"),
            P(("fx", "fy")),
            P(("fx", "fy")),
        ),
        out_specs=P("col", ("fx", "fy")),
        check_vma=False,
    )
```
